512 devices in a mesh: grp: 16 (over z, core), tr: 32 (over x, y).
Axes of the slice: x: 4, y: 8, z: 8, core: 2. Of those that a mesh axis runs over, the one named last changes fastest.
Arguments:
- amplitudes: bfloat16 [512, 1, 32768], P('tr', None, 'grp'), may hold values from -6 to 6
- integrals: bfloat16 [1, 32768, 28672], P(None, 'grp', 'tr'), may hold values from -0.046875 to 0.046875
- slab_count: int32 [1, 16], P(None, 'grp'), may hold values from 512 to 2048, as said below
Outputs:
- ladder: bfloat16 [512, 1, 28672], P('grp', None, 'tr')
The draws below stay inside these ranges and needn't reach their ends.
Inputs may be any that keep to these rules, and one draw needn't show every extreme that they name: `slab_count`: in every irrep block some slab holds exactly 2048 valid pairs.
All inputs are finite; a program needn't handle non-finite values.
Results may differ from the reference program's by a relative error of at most 0.001.
Values may be sent and summed in bfloat16 or wider, within the bound.
No kernel may reach another device: no remote copies, remote signals or barrier semaphores. Data moves between devices by JAX's collectives and lax.ppermute only.
A program may use at most 64 MiB of HBM per device.

```python
import jax
import jax.numpy as jnp

IJ = 512
NBLK = 1
CD_DEV = 2048
SLABS = 16
CD = 32768
AB = 28672


def draw_slab_count(key, part):
    key = jax.random.fold_in(key, 7)
    first, second = jax.random.split(key)
    counts = jax.random.randint(first, (NBLK, SLABS), CD_DEV // 4, CD_DEV + 1)
    full_at = jax.random.randint(second, (NBLK, 1), 0, SLABS)
    position = jnp.arange(SLABS, dtype=jnp.int32)[None, :]
    return jnp.where(position == full_at, CD_DEV, counts).astype(jnp.int32)


def steps_of(own_key, shape, shards, smallest, high):
    factor_of = 1.0
    for dim, shards_of in shards:
        draws = jax.random.uniform(jax.random.fold_in(jax.random.fold_in(own_key, 6), dim), (shards_of,), jnp.float32, smallest / len(shards), high / len(shards))
        factor_of = factor_of * jnp.repeat(jnp.exp(draws), shape[dim] // shards_of).reshape((-1,) + (1,) * (len(shape) - 1 - dim))
    return factor_of


def centred(rng, extent, spread, limit, shards=(), kind=jnp.bfloat16):
    level = steps_of(rng, extent, shards, -0.22, 0.18) if shards else 1.0
    array = jax.random.normal(rng, extent, jnp.float32) * spread * level
    return jnp.minimum(jnp.maximum(array, -limit), limit).astype(kind)


def setup_inputs(seed: int = 0) -> dict:
    key_list = jax.random.split(jax.random.key(seed), 4)
    amplitudes = centred(key_list[0], (IJ, NBLK, CD), 1.0, 6.0, ((0, 32), (2, 16)))
    integrals = centred(key_list[1], (NBLK, CD, AB), (CD // 2) ** -0.5, 0.046875, ((1, 16), (2, 32)))
    slab_count = draw_slab_count(jax.random.fold_in(key_list[3], 71), 0)
    return dict(amplitudes=amplitudes, integrals=integrals, slab_count=slab_count)


def reference(amplitudes, integrals, slab_count):
    position = jnp.arange(CD, dtype=jnp.int32)
    slab_of = position // CD_DEV
    within = position % CD_DEV
    limits = slab_count[:, slab_of]
    valid = within[None, :] < limits
    masked = jnp.where(valid[None, :, :], amplitudes, jnp.zeros_like(amplitudes))
    blocks = []
    for block in range(NBLK):
        blocks.append(jnp.dot(masked[:, block, :], integrals[block], preferred_element_type=jnp.float32))
    return jnp.stack(blocks, axis=1).astype(jnp.bfloat16)
```

```python
import jax
import jax.numpy as jnp
from jax import lax
from jax.sharding import PartitionSpec as P

X, Y, Z = 4, 8, 8
CLASSES = 4


def tr_of(x, y):
    return (x % X) * Y + y % Y


ORDER = [4 * h + 2 * k + b for k in range(2) for h in range(2) for b in range(2)]
CLASS_GROUPS = [[tr_of(c - 2 * y, y) for y in ORDER] for c in range(CLASSES)]


def z_groups():
    groups = []
    for core in range(2):
        for t in range(X * Y):
            c = (t // Y + 2 * (t % Y)) % CLASSES
            planes = [2 * ((c + d) % X) + h for d in range(CLASSES) for h in range(2)]
            groups.append([(2 * z + core) * X * Y + t for z in planes])
    return groups


Z_GROUPS = z_groups()


def from_neighbour(block, dx, dy):
    pairs = [(tr_of(t // Y + dx, t % Y + dy), t) for t in range(X * Y)]
    return lax.ppermute(block, "tr", pairs)


def on_device(amplitudes, integrals, slab_count):
    rows, _, depth = amplitudes.shape
    width = integrals.shape[2]
    column = lax.broadcasted_iota(jnp.int32, (rows, depth), 1)
    masked = jnp.where(column < slab_count[0, 0], amplitudes[:, 0, :], jnp.zeros((), amplitudes.dtype))
    copies = jnp.broadcast_to(masked[None], (8, rows, depth))
    own = lax.all_to_all(copies, "tr", 0, 0, axis_index_groups=CLASS_GROUPS)
    right = from_neighbour(own, 1, 0)
    left = from_neighbour(own, -1, 0)
    up = from_neighbour(own[:4], 0, 1)
    down = from_neighbour(own[4:], 0, -1)
    whole = jnp.concatenate([own[:4], right[:4], up, left[:4], own[4:], right[4:], down, left[4:]], axis=0)
    partial = jnp.dot(whole.reshape(32 * rows, depth), integrals[0], preferred_element_type=jnp.float32)
    both = lax.all_to_all(partial.reshape(2, 16 * rows, width), "grp", 0, 0, axis_index_groups=[[2 * z, 2 * z + 1] for z in range(Z)])
    chip = (both[0] + both[1]).reshape(CLASSES, 2, 2, rows, width)
    second = jnp.concatenate([chip[2:, :, 1], chip[:2, :, 1]], axis=0)
    chip = jnp.stack([chip[:, :, 0], second], axis=2).reshape(Z, 2 * rows, width)
    summed = lax.all_to_all(chip, ("grp", "tr"), 0, 0, axis_index_groups=Z_GROUPS).sum(axis=0)
    return summed.astype(jnp.bfloat16)[:, None, :]


def solution(mesh):
    return jax.shard_map(
        on_device,
        mesh=mesh,
        in_specs=(P("tr", None, "grp"), P(None, "grp", "tr"), P(None, "grp")),
        out_specs=P("grp", None, "tr"),
        check_vma=False,
    )
```

```python
import jax
import jax.numpy as jnp
from jax import lax
from jax.sharding import PartitionSpec as P

X, Y, Z = 4, 8, 8
CLASSES = 4


def tr_of(x, y):
    return (x % X) * Y + y % Y


ORDER = [4 * h + 2 * k + b for k in range(2) for h in range(2) for b in range(2)]
CLASS_GROUPS = [[tr_of(c - 2 * y, y) for y in ORDER] for c in range(CLASSES)]


def z_groups():
    groups = []
    for core in range(2):
        for t in range(X * Y):
            c = (t // Y + 2 * (t % Y)) % CLASSES
            planes = [2 * ((c + d) % X) + h for d in range(CLASSES) for h in range(2)]
            groups.append([(2 * z + core) * X * Y + t for z in planes])
    return groups


Z_GROUPS = z_groups()


def from_neighbour(block, dx, dy):
    pairs = [(tr_of(t // Y + dx, t % Y + dy), t) for t in range(X * Y)]
    return lax.ppermute(block, "tr", pairs)


def on_device(amplitudes, integrals, slab_count):
    rows, _, depth = amplitudes.shape
    width = integrals.shape[2]
    column = lax.broadcasted_iota(jnp.int32, (rows, depth), 1)
    masked = jnp.where(column < slab_count[0, 0], amplitudes[:, 0, :], jnp.zeros((), amplitudes.dtype))
    copies = jnp.broadcast_to(masked[None], (8, rows, depth))
    own = lax.all_to_all(copies, "tr", 0, 0, axis_index_groups=CLASS_GROUPS)
    right = from_neighbour(own, 1, 0)
    left = from_neighbour(own, -1, 0)
    up = from_neighbour(own[:4], 0, 1)
    down = from_neighbour(own[4:], 0, -1)
    mine = lax.rem(lax.axis_index("grp"), 2)

    core0 = mine == 0
    whole = jnp.concatenate([own, right, left, up, down], axis=0).reshape(-1, depth)
    partial = jnp.dot(whole, integrals[0], preferred_element_type=jnp.float32)
    partial = partial.reshape(CLASSES, 2, 4 * rows, width)
    given = lax.ppermute(jnp.where(core0, partial[:, 1], partial[:, 0]), "grp", [(g, g ^ 1) for g in range(2 * Z)])
    total = jnp.where(core0, partial[:, 0], partial[:, 1]) + given
    chip = [total[i].reshape(2, 2, rows, width) for i in (0, 1, 3, 2)]
    paired = [jnp.stack([chip[d][:, 0], chip[(d + 2) % CLASSES][:, 1]], axis=1) for d in range(CLASSES)]
    chip = jnp.stack(paired).reshape(Z, 2 * rows, width)
    summed = lax.all_to_all(chip, ("grp", "tr"), 0, 0, axis_index_groups=Z_GROUPS).sum(axis=0)
    return summed.astype(jnp.bfloat16)[:, None, :]


def solution(mesh):
    return jax.shard_map(
        on_device,
        mesh=mesh,
        in_specs=(P("tr", None, "grp"), P(None, "grp", "tr"), P(None, "grp")),
        out_specs=P("grp", None, "tr"),
        check_vma=False,
    )
```

```python
import jax
import jax.numpy as jnp
from jax import lax
from jax.experimental import pallas as pl
from jax.experimental.pallas import tpu as pltpu
from jax.sharding import PartitionSpec as P

X, Y, Z = 4, 8, 8
CLASSES = 4


def tr_of(x, y):
    return (x % X) * Y + y % Y


ORDER = [4 * h + 2 * k + b for k in range(2) for h in range(2) for b in range(2)]
CLASS_GROUPS = [[tr_of(c - 2 * y, y) for y in ORDER] for c in range(CLASSES)]


def z_groups():
    groups = []
    for core in range(2):
        for t in range(X * Y):
            c = (t // Y + 2 * (t % Y)) % CLASSES
            planes = [2 * ((c + d) % X) + h for d in range(CLASSES) for h in range(2)]
            groups.append([(2 * z + core) * X * Y + t for z in planes])
    return groups


Z_GROUPS = z_groups()


def from_neighbour(block, dx, dy):
    pairs = [(tr_of(t // Y + dx, t % Y + dy), t) for t in range(X * Y)]
    return lax.ppermute(block, "tr", pairs)


def pack(ours_ref, given_ref, out_ref):
    lanes = out_ref.shape[2]
    rows = ours_ref.shape[3]
    groups = ours_ref.shape[4] // lanes
    slot = (0, 1, 3, 2)
    for d in range(CLASSES):
        for h in range(2):
            exponents = []
            for b in range(2):
                at = (slot[(d + 2 * b) % CLASSES], h, b)
                value = ours_ref[at] + given_ref[at]
                top = jnp.max(jnp.abs(value), axis=1, keepdims=True)
                exponent = jnp.ceil(jnp.log2(jnp.maximum(top, 2.0**-100)))
                scaled = jnp.clip(jnp.round(value * jnp.exp2(15.0 - exponent)), -32767.0, 32767.0)
                number = scaled.astype(jnp.int32).astype(jnp.int16)
                for g in range(groups):
                    out_ref[2 * d + h, pl.ds((2 * g + b) * rows, rows), :] = number[:, g * lanes : (g + 1) * lanes]
                exponents.append(jnp.broadcast_to(exponent, (rows, lanes)))
            lower = lax.broadcasted_iota(jnp.int32, (rows, lanes), 1) < lanes // 2
            both = jnp.where(lower, exponents[0], exponents[1])
            out_ref[2 * d + h, pl.ds(2 * groups * rows, rows), :] = both.astype(jnp.int32).astype(jnp.int16)


def unpack_sum(in_ref, out_ref):
    planes, _, lanes = in_ref.shape
    rows = out_ref.shape[0] // 2
    groups = out_ref.shape[1] // lanes
    steps = []
    for p in range(planes):
        exponent = in_ref[p, pl.ds(2 * groups * rows, rows), :].astype(jnp.int32).astype(jnp.float32)
        step = jnp.exp2(exponent - 15.0)
        steps.append((step[:, :1], step[:, lanes // 2 : lanes // 2 + 1]))
    for b in range(2):
        for g in range(groups):
            total = jnp.zeros((rows, lanes), jnp.float32)
            for p in range(planes):
                number = in_ref[p, pl.ds((2 * g + b) * rows, rows), :].astype(jnp.int32).astype(jnp.float32)
                total += number * steps[p][b]
            out_ref[pl.ds(b * rows, rows), g * lanes : (g + 1) * lanes] = total.astype(out_ref.dtype)


LANES = 128


def on_device(amplitudes, integrals, slab_count):
    rows, _, depth = amplitudes.shape
    width = integrals.shape[2]
    column = lax.broadcasted_iota(jnp.int32, (rows, depth), 1)
    masked = jnp.where(column < slab_count[0, 0], amplitudes[:, 0, :], jnp.zeros((), amplitudes.dtype))
    copies = jnp.broadcast_to(masked[None], (8, rows, depth))
    own = lax.all_to_all(copies, "tr", 0, 0, axis_index_groups=CLASS_GROUPS)
    right = from_neighbour(own, 1, 0)
    left = from_neighbour(own, -1, 0)
    up = from_neighbour(own[:4], 0, 1)
    down = from_neighbour(own[4:], 0, -1)
    mine = lax.rem(lax.axis_index("grp"), 2)

    core0 = mine == 0
    whole = jnp.concatenate([own, right, left, up, down], axis=0).reshape(-1, depth)
    partial = jnp.dot(whole, integrals[0], preferred_element_type=jnp.float32)
    partial = partial.reshape(CLASSES, 2, 4 * rows, width)
    given = lax.ppermute(jnp.where(core0, partial[:, 1], partial[:, 0]), "grp", [(g, g ^ 1) for g in range(2 * Z)])
    ours = jnp.where(core0, partial[:, 0], partial[:, 1])
    shape = (CLASSES, 2, 2, rows, width)
    vmem = pl.BlockSpec(memory_space=pltpu.VMEM)
    packed = pl.pallas_call(
        pack,
        out_shape=jax.ShapeDtypeStruct((Z, 2 * rows * (width // LANES) + rows, LANES), jnp.int16),
        in_specs=[vmem, vmem],
        out_specs=vmem,
        compiler_params=pltpu.CompilerParams(vmem_limit_bytes=4 << 20),
        name="pack",
    )(ours.reshape(shape), given.reshape(shape))
    arrived = lax.all_to_all(packed, ("grp", "tr"), 0, 0, axis_index_groups=Z_GROUPS)
    ladder = pl.pallas_call(
        unpack_sum,
        out_shape=jax.ShapeDtypeStruct((2 * rows, width), jnp.bfloat16),
        in_specs=[vmem],
        out_specs=vmem,
        compiler_params=pltpu.CompilerParams(vmem_limit_bytes=2 << 20),
        name="unpack_sum",
    )(arrived)
    return ladder[:, None, :]


def solution(mesh):
    return jax.shard_map(
        on_device,
        mesh=mesh,
        in_specs=(P("tr", None, "grp"), P(None, "grp", "tr"), P(None, "grp")),
        out_specs=P("grp", None, "tr"),
        check_vma=False,
    )
```

```python
import functools

import jax
import jax.numpy as jnp
from jax import lax
from jax.experimental import pallas as pl
from jax.experimental.pallas import tpu as pltpu
from jax.sharding import PartitionSpec as P

X, Y, Z = 4, 8, 8
CLASSES = 4


def tr_of(x, y):
    return (x % X) * Y + y % Y


ORDER = [4 * h + 2 * k + b for k in range(2) for h in range(2) for b in range(2)]
CLASS_GROUPS = [[tr_of(c - 2 * y, y) for y in ORDER] for c in range(CLASSES)]


def z_groups():
    groups = []
    for core in range(2):
        for t in range(X * Y):
            c = (t // Y + 2 * (t % Y)) % CLASSES
            planes = [2 * ((c + d) % X) + h for d in range(CLASSES) for h in range(2)]
            groups.append([(2 * z + core) * X * Y + t for z in planes])
    return groups


Z_GROUPS = z_groups()


def from_neighbour(block, dx, dy):
    pairs = [(tr_of(t // Y + dx, t % Y + dy), t) for t in range(X * Y)]
    return lax.ppermute(block, "tr", pairs)


def multiply(blocks, integrals_ref):
    left = jnp.concatenate([block.reshape(-1, block.shape[-1]) for block in blocks], axis=0)
    return jnp.dot(left, integrals_ref[0], preferred_element_type=jnp.float32)


def this_core():
    return lax.rem(lax.axis_index("grp"), 2)


def near_product(own_ref, right_ref, integrals_ref, ours_ref, theirs_ref):
    core = this_core()
    count = ours_ref.shape[1]
    own, right = own_ref[...], right_ref[...]
    product = multiply([own, right], integrals_ref)
    for d in range(2):
        for k in range(2):
            rows = product[(2 * d + k) * count : (2 * d + k + 1) * count]

            @pl.when(core == k)
            def _():
                ours_ref[d] = rows

            @pl.when(core != k)
            def _():
                theirs_ref[d] = rows


def far_product(side, left_ref, up_ref, down_ref, integrals_ref, out_ref):
    core = lax.rem(this_core() + side, 2)
    half = up_ref.shape[0]
    left = left_ref[pl.ds(core * half, half)]
    across = jnp.where(core == 0, up_ref[...], down_ref[...])
    product = multiply([left, across], integrals_ref)
    count = out_ref.shape[1]
    out_ref[0] = product[:count]
    out_ref[1] = product[count:]


def pack(near_ours_ref, near_given_ref, far_ours_ref, far_given_ref, out_ref):
    lanes = out_ref.shape[2]
    rows = near_ours_ref.shape[1] // 4
    groups = near_ours_ref.shape[2] // lanes
    halves = ((near_ours_ref, near_given_ref), (far_ours_ref, far_given_ref))
    place = ((0, 0), (0, 1), (1, 1), (1, 0))
    for d in range(CLASSES):
        for h in range(2):
            exponents = []
            for b in range(2):
                which, at = place[(d + 2 * b) % CLASSES]
                ours_ref, given_ref = halves[which]
                span = pl.ds((2 * h + b) * rows, rows)
                value = ours_ref[at, span, :] + given_ref[at, span, :]
                top = jnp.max(jnp.abs(value), axis=1, keepdims=True)
                exponent = jnp.ceil(jnp.log2(jnp.maximum(top, 2.0**-100)))
                scaled = jnp.clip(jnp.round(value * jnp.exp2(15.0 - exponent)), -32767.0, 32767.0)
                number = scaled.astype(jnp.int32).astype(jnp.int16)
                for g in range(groups):
                    out_ref[2 * d + h, pl.ds((2 * g + b) * rows, rows), :] = number[:, g * lanes : (g + 1) * lanes]
                exponents.append(jnp.broadcast_to(exponent, (rows, lanes)))
            lower = lax.broadcasted_iota(jnp.int32, (rows, lanes), 1) < lanes // 2
            both = jnp.where(lower, exponents[0], exponents[1])
            out_ref[2 * d + h, pl.ds(2 * groups * rows, rows), :] = both.astype(jnp.int32).astype(jnp.int16)


def unpack_sum(in_ref, out_ref):
    planes, _, lanes = in_ref.shape
    rows = out_ref.shape[0] // 2
    groups = out_ref.shape[1] // lanes
    steps = []
    for p in range(planes):
        exponent = in_ref[p, pl.ds(2 * groups * rows, rows), :].astype(jnp.int32).astype(jnp.float32)
        step = jnp.exp2(exponent - 15.0)
        steps.append((step[:, :1], step[:, lanes // 2 : lanes // 2 + 1]))
    for b in range(2):
        for g in range(groups):
            total = jnp.zeros((rows, lanes), jnp.float32)
            for p in range(planes):
                number = in_ref[p, pl.ds((2 * g + b) * rows, rows), :].astype(jnp.int32).astype(jnp.float32)
                total += number * steps[p][b]
            out_ref[pl.ds(b * rows, rows), g * lanes : (g + 1) * lanes] = total.astype(out_ref.dtype)


LANES = 128
LIMIT_DOT = 8


def call(kernel, shapes, name, limit, flops=0):
    vmem = pl.BlockSpec(memory_space=pltpu.VMEM)
    single = not isinstance(shapes, tuple)

    def run(*operands):
        moved = sum(x.size * x.dtype.itemsize for x in (*operands, *((shapes,) if single else shapes)))
        return pl.pallas_call(
            kernel,
            out_shape=shapes,
            in_specs=[vmem] * len(operands),
            out_specs=vmem if single else (vmem,) * len(shapes),
            compiler_params=pltpu.CompilerParams(vmem_limit_bytes=limit << 20),
            cost_estimate=pl.CostEstimate(flops=flops, bytes_accessed=moved, transcendentals=0),
            name=name,
        )(*operands)

    return run


def on_device(amplitudes, integrals, slab_count):
    rows, _, depth = amplitudes.shape
    width = integrals.shape[2]
    column = lax.broadcasted_iota(jnp.int32, (rows, depth), 1)
    masked = jnp.where(column < slab_count[0, 0], amplitudes[:, 0, :], jnp.zeros((), amplitudes.dtype))
    copies = jnp.broadcast_to(masked[None], (8, rows, depth))
    own = lax.all_to_all(copies, "tr", 0, 0, axis_index_groups=CLASS_GROUPS)
    right = from_neighbour(own, 1, 0)
    left = from_neighbour(own, -1, 0)
    up = from_neighbour(own[:4], 0, 1)
    down = from_neighbour(own[4:], 0, -1)

    side = jax.ShapeDtypeStruct((2, 4 * rows, width), jnp.float32)
    work = 2 * 8 * rows * depth * width
    swap = [(g, g ^ 1) for g in range(2 * Z)]
    near, near_theirs = call(near_product, (side, side), "near", LIMIT_DOT, 2 * work)(own, right, integrals)
    near_given = lax.ppermute(near_theirs, "grp", swap)
    far_theirs = call(functools.partial(far_product, 1), side, "far_theirs", LIMIT_DOT, work)(left, up, down, integrals)
    far_given = lax.ppermute(far_theirs, "grp", swap)
    far = call(functools.partial(far_product, 0), side, "far_ours", LIMIT_DOT, work)(left, up, down, integrals)
    block = jax.ShapeDtypeStruct((Z, 2 * rows * (width // LANES) + rows, LANES), jnp.int16)
    packed = call(pack, block, "pack", 4)(near, near_given, far, far_given)
    arrived = lax.all_to_all(packed, ("grp", "tr"), 0, 0, axis_index_groups=Z_GROUPS)
    ladder = call(unpack_sum, jax.ShapeDtypeStruct((2 * rows, width), jnp.bfloat16), "unpack_sum", 2)(arrived)
    return ladder[:, None, :]


def solution(mesh):
    return jax.shard_map(
        on_device,
        mesh=mesh,
        in_specs=(P("tr", None, "grp"), P(None, "grp", "tr"), P(None, "grp")),
        out_specs=P("grp", None, "tr"),
        check_vma=False,
    )
```

```python
import functools

import jax
import jax.numpy as jnp
from jax import lax
from jax.experimental import pallas as pl
from jax.experimental.pallas import tpu as pltpu
from jax.sharding import PartitionSpec as P

X, Y, Z = 4, 8, 8
CLASSES = 4


def tr_of(x, y):
    return (x % X) * Y + y % Y


ORDER = [4 * h + 2 * k + b for k in range(2) for h in range(2) for b in range(2)]
CLASS_GROUPS = [[tr_of(c - 2 * y, y) for y in ORDER] for c in range(CLASSES)]


def z_groups():
    groups = []
    for core in range(2):
        for t in range(X * Y):
            c = (t // Y + 2 * (t % Y)) % CLASSES
            planes = [2 * ((c + d) % X) + h for d in range(CLASSES) for h in range(2)]
            groups.append([(2 * z + core) * X * Y + t for z in planes])
    return groups


Z_GROUPS = z_groups()


def from_neighbour(block, dx, dy):
    pairs = [(tr_of(t // Y + dx, t % Y + dy), t) for t in range(X * Y)]
    return lax.ppermute(block, "tr", pairs)


def multiply(blocks, integrals_ref):
    left = jnp.concatenate([block.reshape(-1, block.shape[-1]) for block in blocks], axis=0)
    return jnp.dot(left, integrals_ref[0], preferred_element_type=jnp.float32)


def this_core():
    return lax.rem(lax.axis_index("grp"), 2)


def split(own_ref, low_ref, high_ref):
    low_ref[...] = own_ref[:4]
    high_ref[...] = own_ref[4:]


def near_product(own_ref, right_ref, integrals_ref, ours_ref, theirs_ref):
    core = this_core()
    count = ours_ref.shape[1]
    own, right = own_ref[...], right_ref[...]
    product = multiply([own, right], integrals_ref)
    for d in range(2):
        for k in range(2):
            rows = product[(2 * d + k) * count : (2 * d + k + 1) * count]

            @pl.when(core == k)
            def _():
                ours_ref[d] = rows

            @pl.when(core != k)
            def _():
                theirs_ref[d] = rows


def far_product(side, left_ref, up_ref, down_ref, integrals_ref, out_ref):
    core = lax.rem(this_core() + side, 2)
    half = up_ref.shape[0]
    left = left_ref[pl.ds(core * half, half)]
    across = jnp.where(core == 0, up_ref[...], down_ref[...])
    product = multiply([left, across], integrals_ref)
    count = out_ref.shape[1]
    out_ref[0] = product[:count]
    out_ref[1] = product[count:]


def pack(near_ours_ref, near_given_ref, far_ours_ref, far_given_ref, out_ref):
    lanes = out_ref.shape[2]
    rows = near_ours_ref.shape[1] // 4
    groups = near_ours_ref.shape[2] // lanes
    halves = ((near_ours_ref, near_given_ref), (far_ours_ref, far_given_ref))
    place = ((0, 0), (0, 1), (1, 1), (1, 0))
    for d in range(CLASSES):
        for h in range(2):
            exponents = []
            for b in range(2):
                which, at = place[(d + 2 * b) % CLASSES]
                ours_ref, given_ref = halves[which]
                span = pl.ds((2 * h + b) * rows, rows)
                value = ours_ref[at, span, :] + given_ref[at, span, :]
                top = jnp.max(jnp.abs(value), axis=1, keepdims=True)
                exponent = jnp.ceil(jnp.log2(jnp.maximum(top, 2.0**-100)))
                scaled = jnp.clip(jnp.round(value * jnp.exp2(15.0 - exponent)), -32767.0, 32767.0)
                number = scaled.astype(jnp.int32).astype(jnp.int16)
                for g in range(groups):
                    out_ref[2 * d + h, pl.ds((2 * g + b) * rows, rows), :] = number[:, g * lanes : (g + 1) * lanes]
                exponents.append(jnp.broadcast_to(exponent, (rows, lanes)))
            lower = lax.broadcasted_iota(jnp.int32, (rows, lanes), 1) < lanes // 2
            both = jnp.where(lower, exponents[0], exponents[1])
            out_ref[2 * d + h, pl.ds(2 * groups * rows, rows), :] = both.astype(jnp.int32).astype(jnp.int16)


def unpack_sum(in_ref, out_ref):
    planes, _, lanes = in_ref.shape
    rows = out_ref.shape[0] // 2
    groups = out_ref.shape[1] // lanes
    steps = []
    for p in range(planes):
        exponent = in_ref[p, pl.ds(2 * groups * rows, rows), :].astype(jnp.int32).astype(jnp.float32)
        step = jnp.exp2(exponent - 15.0)
        steps.append((step[:, :1], step[:, lanes // 2 : lanes // 2 + 1]))
    for b in range(2):
        for g in range(groups):
            total = jnp.zeros((rows, lanes), jnp.float32)
            for p in range(planes):
                number = in_ref[p, pl.ds((2 * g + b) * rows, rows), :].astype(jnp.int32).astype(jnp.float32)
                total += number * steps[p][b]
            out_ref[pl.ds(b * rows, rows), g * lanes : (g + 1) * lanes] = total.astype(out_ref.dtype)


LANES = 128
LIMIT_DOT = 8


def call(kernel, shapes, name, limit, flops=0):
    vmem = pl.BlockSpec(memory_space=pltpu.VMEM)
    single = not isinstance(shapes, tuple)

    def run(*operands):
        moved = sum(x.size * x.dtype.itemsize for x in (*operands, *((shapes,) if single else shapes)))
        return pl.pallas_call(
            kernel,
            out_shape=shapes,
            in_specs=[vmem] * len(operands),
            out_specs=vmem if single else (vmem,) * len(shapes),
            compiler_params=pltpu.CompilerParams(vmem_limit_bytes=limit << 20),
            cost_estimate=pl.CostEstimate(flops=flops, bytes_accessed=moved, transcendentals=0),
            name=name,
        )(*operands)

    return run


def on_device(amplitudes, integrals, slab_count):
    rows, _, depth = amplitudes.shape
    width = integrals.shape[2]
    column = lax.broadcasted_iota(jnp.int32, (rows, depth), 1)
    masked = jnp.where(column < slab_count[0, 0], amplitudes[:, 0, :], jnp.zeros((), amplitudes.dtype))
    copies = jnp.broadcast_to(masked[None], (8, rows, depth))
    own = lax.all_to_all(copies, "tr", 0, 0, axis_index_groups=CLASS_GROUPS)
    right = from_neighbour(own, 1, 0)
    left = from_neighbour(own, -1, 0)
    half = jax.ShapeDtypeStruct((4, rows, depth), own.dtype)
    low, high = call(split, (half, half), "split", 4, 4000000000)(own)
    up = from_neighbour(low, 0, 1)
    down = from_neighbour(high, 0, -1)

    side = jax.ShapeDtypeStruct((2, 4 * rows, width), jnp.float32)
    work = 2 * 8 * rows * depth * width
    swap = [(g, g ^ 1) for g in range(2 * Z)]
    near, near_theirs = call(near_product, (side, side), "near", LIMIT_DOT, 2 * work)(own, right, integrals)
    near_given = lax.ppermute(near_theirs, "grp", swap)
    far_theirs = call(functools.partial(far_product, 1), side, "far_theirs", LIMIT_DOT, work)(left, up, down, integrals)
    far_given = lax.ppermute(far_theirs, "grp", swap)
    far = call(functools.partial(far_product, 0), side, "far_ours", LIMIT_DOT, work)(left, up, down, integrals)
    block = jax.ShapeDtypeStruct((Z, 2 * rows * (width // LANES) + rows, LANES), jnp.int16)
    packed = call(pack, block, "pack", 4)(near, near_given, far, far_given)
    arrived = lax.all_to_all(packed, ("grp", "tr"), 0, 0, axis_index_groups=Z_GROUPS)
    ladder = call(unpack_sum, jax.ShapeDtypeStruct((2 * rows, width), jnp.bfloat16), "unpack_sum", 2)(arrived)
    return ladder[:, None, :]


def solution(mesh):
    return jax.shard_map(
        on_device,
        mesh=mesh,
        in_specs=(P("tr", None, "grp"), P(None, "grp", "tr"), P(None, "grp")),
        out_specs=P("grp", None, "tr"),
        check_vma=False,
    )
```

```python
import functools

import jax
import jax.numpy as jnp
from jax import lax
from jax.experimental import pallas as pl
from jax.experimental.pallas import tpu as pltpu
from jax.sharding import PartitionSpec as P

X, Y, Z = 4, 8, 8
CLASSES = 4


def tr_of(x, y):
    return (x % X) * Y + y % Y


ORDER = (0, 2, 4, 6, 1, 3, 5, 7)
CLASS_GROUPS = [[tr_of(c - 2 * y, y) for y in ORDER] for c in range(CLASSES)]

FOLD = (0, 7, 1, 6, 2, 5, 3, 4)


def z_groups():
    groups = []
    for core in range(2):
        for t in range(X * Y):
            c = (t // Y + 2 * (t % Y)) % CLASSES
            groups.append([(2 * ((2 * c + plane) % Z) + core) * X * Y + t for plane in FOLD])
    return groups


Z_GROUPS = z_groups()


def exchange(block, dx, dy):
    pairs = []
    for t in range(X * Y):
        x, y = t // Y, t % Y
        sign = 1 - 2 * ((x if dx else y) % 2)
        pairs.append((tr_of(x + sign * dx, y + sign * dy), t))
    return lax.ppermute(block, "tr", pairs)


def multiply(blocks, integrals_ref):
    left = jnp.concatenate([block.reshape(-1, block.shape[-1]) for block in blocks], axis=0)
    return jnp.dot(left, integrals_ref[0], preferred_element_type=jnp.float32)


def this_core():
    return lax.rem(lax.axis_index("grp"), 2)


def split(own_ref, low_ref, high_ref):
    low_ref[...] = own_ref[:MOST]
    high_ref[...] = own_ref[MOST:]


def near_product(own_ref, right_ref, integrals_ref, ours_ref, theirs_ref):
    core = this_core()
    rows = own_ref.shape[1]
    product = multiply([own_ref[...], right_ref[...]], integrals_ref)
    for d in range(2):
        for block in range(8):
            start = (8 * d + block) * rows
            values = product[start : start + rows]
            span = pl.ds(block // 2 * rows, rows)

            @pl.when(core == block % 2)
            def _():
                ours_ref[d, span] = values

            @pl.when(core != block % 2)
            def _():
                theirs_ref[d, span] = values


def far_product(side, left_ref, up_ref, down_ref, integrals_ref, out_ref):
    core = lax.rem(this_core() + side, 2)
    blocks = [left_ref[core + 2 * i] for i in range(4)]
    across = [up_ref[i] for i in range(MOST)] + [down_ref[i] for i in range(8 - MOST)]
    blocks += [jnp.where(core == 0, across[2 * i], across[2 * i + 1]) for i in range(4)]
    product = multiply(blocks, integrals_ref)
    count = out_ref.shape[1]
    out_ref[0] = product[:count]
    out_ref[1] = product[count:]


def pack(near_ours_ref, near_given_ref, far_ours_ref, far_given_ref, out_ref):
    lanes = out_ref.shape[2]
    rows = near_ours_ref.shape[1] // 4
    groups = near_ours_ref.shape[2] // lanes
    ours = [near_ours_ref.at[0], near_ours_ref.at[1], far_ours_ref.at[1], far_ours_ref.at[0]]
    given = [near_given_ref.at[0], near_given_ref.at[1], far_given_ref.at[1], far_given_ref.at[0]]
    odd = lax.rem(lax.axis_index("tr") // Y, 2)
    for way in range(2):

        @pl.when(odd == way)
        def _():
            for d in range(CLASSES):
                for h in range(2):
                    place_out = FOLD.index(2 * d + h)
                    exponents = []
                    for b in range(2):
                        at = (1 - 2 * way) * ((d + 2 * b) % CLASSES)
                        span = pl.ds((2 * b + h) * rows, rows)
                        value = ours[at][span, :] + given[at][span, :]
                        top = jnp.max(jnp.abs(value), axis=1, keepdims=True)
                        exponent = jnp.ceil(jnp.log2(jnp.maximum(top, 2.0**-100)))
                        scaled = jnp.clip(jnp.round(value * jnp.exp2(15.0 - exponent)), -32767.0, 32767.0)
                        number = scaled.astype(jnp.int32).astype(jnp.int16)
                        for g in range(groups):
                            lane = pl.ds((2 * g + b) * rows, rows)
                            out_ref[place_out, lane, :] = number[:, g * lanes : (g + 1) * lanes]
                        exponents.append(jnp.broadcast_to(exponent, (rows, lanes)))
                    lower = lax.broadcasted_iota(jnp.int32, (rows, lanes), 1) < lanes // 2
                    both = jnp.where(lower, exponents[0], exponents[1])
                    out_ref[place_out, pl.ds(2 * groups * rows, rows), :] = both.astype(jnp.int32).astype(jnp.int16)


def unpack_sum(in_ref, out_ref):
    planes, _, lanes = in_ref.shape
    rows = out_ref.shape[0] // 2
    groups = out_ref.shape[1] // lanes
    steps = []
    for p in range(planes):
        exponent = in_ref[p, pl.ds(2 * groups * rows, rows), :].astype(jnp.int32).astype(jnp.float32)
        step = jnp.exp2(exponent - 15.0)
        steps.append((step[:, :1], step[:, lanes // 2 : lanes // 2 + 1]))
    for b in range(2):
        for g in range(groups):
            total = jnp.zeros((rows, lanes), jnp.float32)
            for p in range(planes):
                number = in_ref[p, pl.ds((2 * g + b) * rows, rows), :].astype(jnp.int32).astype(jnp.float32)
                total += number * steps[p][b]
            out_ref[pl.ds(b * rows, rows), g * lanes : (g + 1) * lanes] = total.astype(out_ref.dtype)


LANES = 128
LIMIT_DOT = 8
MOST = 5


def call(kernel, shapes, name, limit, flops=0):
    vmem = pl.BlockSpec(memory_space=pltpu.VMEM)
    single = not isinstance(shapes, tuple)

    def run(*operands):
        moved = sum(x.size * x.dtype.itemsize for x in (*operands, *((shapes,) if single else shapes)))
        return pl.pallas_call(
            kernel,
            out_shape=shapes,
            in_specs=[vmem] * len(operands),
            out_specs=vmem if single else (vmem,) * len(shapes),
            compiler_params=pltpu.CompilerParams(vmem_limit_bytes=limit << 20),
            cost_estimate=pl.CostEstimate(flops=flops, bytes_accessed=moved, transcendentals=0),
            name=name,
        )(*operands)

    return run


def on_device(amplitudes, integrals, slab_count):
    rows, _, depth = amplitudes.shape
    width = integrals.shape[2]
    column = lax.broadcasted_iota(jnp.int32, (rows, depth), 1)
    masked = jnp.where(column < slab_count[0, 0], amplitudes[:, 0, :], jnp.zeros((), amplitudes.dtype))
    copies = jnp.broadcast_to(masked[None], (8, rows, depth))
    own = lax.all_to_all(copies, "tr", 0, 0, axis_index_groups=CLASS_GROUPS)
    right = exchange(own, 1, 0)
    left = exchange(own, -1, 0)
    parts = tuple(jax.ShapeDtypeStruct((n, rows, depth), own.dtype) for n in (MOST, 8 - MOST))
    low, high = call(split, parts, "split", 4, 4000000000)(own)
    up = exchange(low, 0, 1)
    down = exchange(high, 0, -1)

    side = jax.ShapeDtypeStruct((2, 4 * rows, width), jnp.float32)
    work = 2 * 8 * rows * depth * width
    swap = [(g, g ^ 1) for g in range(2 * Z)]
    near, near_theirs = call(near_product, (side, side), "near", LIMIT_DOT, 2 * work)(own, right, integrals)
    near_given = lax.ppermute(near_theirs, "grp", swap)
    far_theirs = call(functools.partial(far_product, 1), side, "far_theirs", LIMIT_DOT, work)(left, up, down, integrals)
    far_given = lax.ppermute(far_theirs, "grp", swap)
    far = call(functools.partial(far_product, 0), side, "far_ours", LIMIT_DOT, work)(left, up, down, integrals)
    block = jax.ShapeDtypeStruct((Z, 2 * rows * (width // LANES) + rows, LANES), jnp.int16)
    packed = call(pack, block, "pack", 4)(near, near_given, far, far_given)
    arrived = lax.all_to_all(packed, ("grp", "tr"), 0, 0, axis_index_groups=Z_GROUPS)
    ladder = call(unpack_sum, jax.ShapeDtypeStruct((2 * rows, width), jnp.bfloat16), "unpack_sum", 2)(arrived)
    return ladder[:, None, :]


def solution(mesh):
    return jax.shard_map(
        on_device,
        mesh=mesh,
        in_specs=(P("tr", None, "grp"), P(None, "grp", "tr"), P(None, "grp")),
        out_specs=P("grp", None, "tr"),
        check_vma=False,
    )
```

```python
import functools

import jax
import jax.numpy as jnp
from jax import lax
from jax.experimental import pallas as pl
from jax.experimental.pallas import tpu as pltpu
from jax.sharding import PartitionSpec as P

X, Y, Z = 4, 8, 8
CLASSES = 4


def tr_of(x, y):
    return (x % X) * Y + y % Y


ORDER = (0, 2, 4, 6, 1, 3, 5, 7)
CLASS_GROUPS = [[tr_of(c - 2 * y, y) for y in ORDER] for c in range(CLASSES)]

FOLD = (0, 7, 1, 6, 2, 5, 3, 4)


def z_groups():
    groups = []
    for core in range(2):
        for t in range(X * Y):
            c = (t // Y + 2 * (t % Y)) % CLASSES
            groups.append([(2 * ((2 * c + plane) % Z) + core) * X * Y + t for plane in FOLD])
    return groups


Z_GROUPS = z_groups()


def exchange(block, dx, dy, flip=0):
    pairs = []
    for g in range(2 * Z):
        for t in range(X * Y):
            x, y = t // Y, t % Y
            sign = 1 - 2 * (((x if dx else y) + flip * g) % 2)
            pairs.append((g * X * Y + tr_of(x + sign * dx, y + sign * dy), g * X * Y + t))
    return lax.ppermute(block, ("grp", "tr"), pairs)


def multiply(blocks, integrals_ref):
    left = jnp.concatenate([block.reshape(-1, block.shape[-1]) for block in blocks], axis=0)
    return jnp.dot(left, integrals_ref[0], preferred_element_type=jnp.float32)


def this_core():
    return lax.rem(lax.axis_index("grp"), 2)


def split(own_ref, copy_ref):
    copy_ref[...] = own_ref[...]


def near_product(own_ref, right_ref, integrals_ref, ours_ref, theirs_ref):
    core = this_core()
    rows = own_ref.shape[1]
    product = multiply([own_ref[...], right_ref[...]], integrals_ref)
    for d in range(2):
        for block in range(8):
            start = (8 * d + block) * rows
            values = product[start : start + rows]
            span = pl.ds(block // 2 * rows, rows)

            @pl.when(core == block % 2)
            def _():
                ours_ref[d, span] = values

            @pl.when(core != block % 2)
            def _():
                theirs_ref[d, span] = values


def far_product(side, left_ref, up_ref, integrals_ref, out_ref):
    core = lax.rem(this_core() + side, 2)
    blocks = [left_ref[core + 2 * i] for i in range(4)]
    blocks += [up_ref[core + 2 * i] for i in range(4)]
    product = multiply(blocks, integrals_ref)
    count = out_ref.shape[1]
    out_ref[0] = product[:count]
    out_ref[1] = product[count:]


def pack(near_ours_ref, near_given_ref, far_ours_ref, far_given_ref, out_ref):
    lanes = out_ref.shape[2]
    rows = near_ours_ref.shape[1] // 4
    groups = near_ours_ref.shape[2] // lanes
    ours = [near_ours_ref.at[0], near_ours_ref.at[1], far_ours_ref.at[1], far_ours_ref.at[0]]
    given = [near_given_ref.at[0], near_given_ref.at[1], far_given_ref.at[1], far_given_ref.at[0]]
    odd = lax.rem(lax.axis_index("tr") // Y, 2)
    for way in range(2):

        @pl.when(odd == way)
        def _():
            for d in range(CLASSES):
                for h in range(2):
                    place_out = FOLD.index(2 * d + h)
                    exponents = []
                    for b in range(2):
                        at = (1 - 2 * way) * ((d + 2 * b) % CLASSES)
                        span = pl.ds((2 * b + h) * rows, rows)
                        value = ours[at][span, :] + given[at][span, :]
                        top = jnp.max(jnp.abs(value), axis=1, keepdims=True)
                        exponent = jnp.ceil(jnp.log2(jnp.maximum(top, 2.0**-110)))
                        scaled = jnp.clip(jnp.round(value * jnp.exp2(15.0 - exponent)), -32767.0, 32767.0)
                        number = scaled.astype(jnp.int32).astype(jnp.int16)
                        for g in range(groups):
                            lane = pl.ds((2 * g + b) * rows, rows)
                            out_ref[place_out, lane, :] = number[:, g * lanes : (g + 1) * lanes]
                        exponents.append(jnp.broadcast_to(exponent, (rows, lanes)))
                    lower = lax.broadcasted_iota(jnp.int32, (rows, lanes), 1) < lanes // 2
                    both = jnp.where(lower, exponents[0], exponents[1])
                    out_ref[place_out, pl.ds(2 * groups * rows, rows), :] = both.astype(jnp.int32).astype(jnp.int16)


def unpack_sum(in_ref, out_ref):
    planes, _, lanes = in_ref.shape
    rows = out_ref.shape[0] // 2
    groups = out_ref.shape[1] // lanes
    steps = []
    for p in range(planes):
        exponent = in_ref[p, pl.ds(2 * groups * rows, rows), :].astype(jnp.int32).astype(jnp.float32)
        step = jnp.exp2(exponent - 15.0)
        steps.append((step[:, :1], step[:, lanes // 2 : lanes // 2 + 1]))
    for b in range(2):
        for g in range(groups):
            total = jnp.zeros((rows, lanes), jnp.float32)
            for p in range(planes):
                number = in_ref[p, pl.ds((2 * g + b) * rows, rows), :].astype(jnp.int32).astype(jnp.float32)
                total += number * steps[p][b]
            out_ref[pl.ds(b * rows, rows), g * lanes : (g + 1) * lanes] = total.astype(out_ref.dtype)


LANES = 128
LIMIT_DOT = 8
MOST = 5


def call(kernel, shapes, name, limit, flops=0):
    vmem = pl.BlockSpec(memory_space=pltpu.VMEM)
    single = not isinstance(shapes, tuple)

    def run(*operands):
        moved = sum(x.size * x.dtype.itemsize for x in (*operands, *((shapes,) if single else shapes)))
        return pl.pallas_call(
            kernel,
            out_shape=shapes,
            in_specs=[vmem] * len(operands),
            out_specs=vmem if single else (vmem,) * len(shapes),
            compiler_params=pltpu.CompilerParams(vmem_limit_bytes=limit << 20),
            cost_estimate=pl.CostEstimate(flops=flops, bytes_accessed=moved, transcendentals=0),
            name=name,
        )(*operands)

    return run


def on_device(amplitudes, integrals, slab_count):
    rows, _, depth = amplitudes.shape
    width = integrals.shape[2]
    column = lax.broadcasted_iota(jnp.int32, (rows, depth), 1)
    masked = jnp.where(column < slab_count[0, 0], amplitudes[:, 0, :], jnp.zeros((), amplitudes.dtype))
    copies = jnp.broadcast_to(masked[None], (8, rows, depth))
    own = lax.all_to_all(copies, "tr", 0, 0, axis_index_groups=CLASS_GROUPS)
    right = exchange(own, 1, 0)
    left = exchange(own, -1, 0)
    parts = jax.ShapeDtypeStruct(own.shape, own.dtype)
    copy = call(split, parts, "split", 4, 4000000000)(own)
    up = exchange(copy, 0, 1, 1)

    side = jax.ShapeDtypeStruct((2, 4 * rows, width), jnp.float32)
    work = 2 * 8 * rows * depth * width
    swap = [(g, g ^ 1) for g in range(2 * Z)]
    near, near_theirs = call(near_product, (side, side), "near", LIMIT_DOT, 2 * work)(own, right, integrals)
    near_given = lax.ppermute(near_theirs, "grp", swap)
    far_theirs = call(functools.partial(far_product, 1), side, "far_theirs", LIMIT_DOT, work)(left, up, integrals)
    far_given = lax.ppermute(far_theirs, "grp", swap)
    far = call(functools.partial(far_product, 0), side, "far_ours", LIMIT_DOT, work)(left, up, integrals)
    block = jax.ShapeDtypeStruct((Z, 2 * rows * (width // LANES) + rows, LANES), jnp.int16)
    packed = call(pack, block, "pack", 4)(near, near_given, far, far_given)
    arrived = lax.all_to_all(packed, ("grp", "tr"), 0, 0, axis_index_groups=Z_GROUPS)
    ladder = call(unpack_sum, jax.ShapeDtypeStruct((2 * rows, width), jnp.bfloat16), "unpack_sum", 2)(arrived)
    return ladder[:, None, :]


def solution(mesh):
    return jax.shard_map(
        on_device,
        mesh=mesh,
        in_specs=(P("tr", None, "grp"), P(None, "grp", "tr"), P(None, "grp")),
        out_specs=P("grp", None, "tr"),
        check_vma=False,
    )
```

```python
import functools

import jax
import jax.numpy as jnp
from jax import lax
from jax.experimental import pallas as pl
from jax.experimental.pallas import tpu as pltpu
from jax.sharding import PartitionSpec as P

X, Y, Z = 4, 8, 8
CLASSES = 4


def tr_of(x, y):
    return (x % X) * Y + y % Y


ORDER = (0, 2, 4, 6, 1, 3, 5, 7)
CLASS_GROUPS = [[tr_of(c - 2 * y, y) for y in ORDER] for c in range(CLASSES)]

FOLD = (0, 7, 1, 6, 2, 5, 3, 4)


def z_groups():
    groups = []
    for core in range(2):
        for t in range(X * Y):
            c = (t // Y + 2 * (t % Y)) % CLASSES
            groups.append([(2 * ((2 * c + plane) % Z) + core) * X * Y + t for plane in FOLD])
    return groups


Z_GROUPS = z_groups()


def exchange(block, dx, dy, flip=0):
    pairs = []
    for g in range(2 * Z):
        for t in range(X * Y):
            x, y = t // Y, t % Y
            sign = 1 - 2 * (((x if dx else y) + flip * g) % 2)
            pairs.append((g * X * Y + tr_of(x + sign * dx, y + sign * dy), g * X * Y + t))
    return lax.ppermute(block, ("grp", "tr"), pairs)


def multiply(blocks, integrals_ref):
    left = jnp.concatenate([block.reshape(-1, block.shape[-1]) for block in blocks], axis=0)
    return jnp.dot(left, integrals_ref[0], preferred_element_type=jnp.float32)


def this_core():
    return lax.rem(lax.axis_index("grp"), 2)


def copy_own(own_ref, copy_ref):
    copy_ref[...] = own_ref[...]


def near_product(own_ref, right_ref, integrals_ref, ours_ref, theirs_ref):
    core = this_core()
    rows = own_ref.shape[1]
    product = multiply([own_ref[...], right_ref[...]], integrals_ref)
    for d in range(2):
        for block in range(8):
            start = (8 * d + block) * rows
            values = product[start : start + rows]
            span = pl.ds(block // 2 * rows, rows)

            @pl.when(core == block % 2)
            def _():
                ours_ref[d, span] = values

            @pl.when(core != block % 2)
            def _():
                theirs_ref[d, span] = values


def far_product(side, left_ref, up_ref, integrals_ref, out_ref):
    core = lax.rem(this_core() + side, 2)
    blocks = [left_ref[core + 2 * i] for i in range(4)]
    blocks += [up_ref[core + 2 * i] for i in range(4)]
    product = multiply(blocks, integrals_ref)
    count = out_ref.shape[1]
    out_ref[0] = product[:count]
    out_ref[1] = product[count:]


def pack(near_ours_ref, near_given_ref, far_ours_ref, far_given_ref, out_ref):
    lanes = out_ref.shape[2]
    rows = near_ours_ref.shape[1] // 4
    groups = near_ours_ref.shape[2] // lanes
    ours = [near_ours_ref.at[0], near_ours_ref.at[1], far_ours_ref.at[1], far_ours_ref.at[0]]
    given = [near_given_ref.at[0], near_given_ref.at[1], far_given_ref.at[1], far_given_ref.at[0]]
    odd = lax.rem(lax.axis_index("tr") // Y, 2)
    for way in range(2):

        @pl.when(odd == way)
        def _():
            for d in range(CLASSES):
                for h in range(2):
                    place_out = FOLD.index(2 * d + h)
                    exponents = []
                    for b in range(2):
                        at = (1 - 2 * way) * ((d + 2 * b) % CLASSES)
                        span = pl.ds((2 * b + h) * rows, rows)
                        value = ours[at][span, :] + given[at][span, :]
                        top = jnp.max(jnp.abs(value), axis=1, keepdims=True)
                        exponent = jnp.ceil(FINE * jnp.log2(jnp.maximum(top, 2.0**-110)))
                        scaled = jnp.clip(jnp.round(value * jnp.exp2(15.0 - exponent / FINE)), -32767.0, 32767.0)
                        number = scaled.astype(jnp.int32).astype(jnp.int16)
                        for g in range(groups):
                            lane = pl.ds((2 * g + b) * rows, rows)
                            out_ref[place_out, lane, :] = number[:, g * lanes : (g + 1) * lanes]
                        exponents.append(jnp.broadcast_to(exponent, (rows, lanes)))
                    lower = lax.broadcasted_iota(jnp.int32, (rows, lanes), 1) < lanes // 2
                    both = jnp.where(lower, exponents[0], exponents[1])
                    out_ref[place_out, pl.ds(2 * groups * rows, rows), :] = both.astype(jnp.int32).astype(jnp.int16)


def unpack_sum(in_ref, out_ref):
    planes, _, lanes = in_ref.shape
    rows = out_ref.shape[0] // 2
    groups = out_ref.shape[1] // lanes
    steps = []
    for p in range(planes):
        exponent = in_ref[p, pl.ds(2 * groups * rows, rows), :].astype(jnp.int32).astype(jnp.float32)
        step = jnp.exp2(exponent / FINE - 15.0)
        steps.append((step[:, :1], step[:, lanes // 2 : lanes // 2 + 1]))
    for b in range(2):
        for g in range(groups):
            total = jnp.zeros((rows, lanes), jnp.float32)
            for p in range(planes):
                number = in_ref[p, pl.ds((2 * g + b) * rows, rows), :].astype(jnp.int32).astype(jnp.float32)
                total += number * steps[p][b]
            out_ref[pl.ds(b * rows, rows), g * lanes : (g + 1) * lanes] = total.astype(out_ref.dtype)


LANES = 128
FINE = 64
LIMIT_DOT = 8


def call(kernel, shapes, name, limit, flops=0):
    vmem = pl.BlockSpec(memory_space=pltpu.VMEM)
    single = not isinstance(shapes, tuple)

    def run(*operands):
        moved = sum(x.size * x.dtype.itemsize for x in (*operands, *((shapes,) if single else shapes)))
        return pl.pallas_call(
            kernel,
            out_shape=shapes,
            in_specs=[vmem] * len(operands),
            out_specs=vmem if single else (vmem,) * len(shapes),
            compiler_params=pltpu.CompilerParams(vmem_limit_bytes=limit << 20),
            cost_estimate=pl.CostEstimate(flops=flops, bytes_accessed=moved, transcendentals=0),
            name=name,
        )(*operands)

    return run


def on_device(amplitudes, integrals, slab_count):
    rows, _, depth = amplitudes.shape
    width = integrals.shape[2]
    column = lax.broadcasted_iota(jnp.int32, (rows, depth), 1)
    masked = jnp.where(column < slab_count[0, 0], amplitudes[:, 0, :], jnp.zeros((), amplitudes.dtype))
    copies = jnp.broadcast_to(masked[None], (8, rows, depth))
    own = lax.all_to_all(copies, "tr", 0, 0, axis_index_groups=CLASS_GROUPS)
    right = exchange(own, 1, 0)
    left = exchange(own, -1, 0)
    parts = jax.ShapeDtypeStruct(own.shape, own.dtype)
    copy = call(copy_own, parts, "copy_own", 4, 4000000000)(own)
    up = exchange(copy, 0, 1, 1)

    side = jax.ShapeDtypeStruct((2, 4 * rows, width), jnp.float32)
    work = 2 * 8 * rows * depth * width
    swap = [(g, g ^ 1) for g in range(2 * Z)]
    near, near_theirs = call(near_product, (side, side), "near", LIMIT_DOT, 2 * work)(own, right, integrals)
    near_given = lax.ppermute(near_theirs, "grp", swap)
    far_theirs = call(functools.partial(far_product, 1), side, "far_theirs", LIMIT_DOT, work)(left, up, integrals)
    far_given = lax.ppermute(far_theirs, "grp", swap)
    far = call(functools.partial(far_product, 0), side, "far_ours", LIMIT_DOT, work)(left, up, integrals)
    block = jax.ShapeDtypeStruct((Z, 2 * rows * (width // LANES) + rows, LANES), jnp.int16)
    packed = call(pack, block, "pack", 4)(near, near_given, far, far_given)
    arrived = lax.all_to_all(packed, ("grp", "tr"), 0, 0, axis_index_groups=Z_GROUPS)
    ladder = call(unpack_sum, jax.ShapeDtypeStruct((2 * rows, width), jnp.bfloat16), "unpack_sum", 2)(arrived)
    return ladder[:, None, :]


def solution(mesh):
    return jax.shard_map(
        on_device,
        mesh=mesh,
        in_specs=(P("tr", None, "grp"), P(None, "grp", "tr"), P(None, "grp")),
        out_specs=P("grp", None, "tr"),
        check_vma=False,
    )
```

```python
import functools

import jax
import jax.numpy as jnp
from jax import lax
from jax.experimental import pallas as pl
from jax.experimental.pallas import tpu as pltpu
from jax.sharding import PartitionSpec as P

X, Y, Z = 4, 8, 8
CLASSES = 4


def tr_of(x, y):
    return (x % X) * Y + y % Y


ORDER = (0, 7, 1, 6, 2, 5, 3, 4)
PLACES = [[ORDER.index(4 * h + 2 * k + b) for b in range(2) for h in range(2)] for k in range(2)]
CLASS_GROUPS = [[tr_of(c - 2 * y, y) for y in ORDER] for c in range(CLASSES)]

FOLD = (0, 7, 1, 6, 2, 5, 3, 4)


def z_groups():
    groups = []
    for core in range(2):
        for t in range(X * Y):
            c = (t // Y + 2 * (t % Y)) % CLASSES
            groups.append([(2 * ((2 * c + plane) % Z) + core) * X * Y + t for plane in FOLD])
    return groups


Z_GROUPS = z_groups()


def exchange(block, dx, dy, flip=0):
    pairs = []
    for g in range(2 * Z):
        for t in range(X * Y):
            x, y = t // Y, t % Y
            sign = 1 - 2 * (((x if dx else y) + flip * g) % 2)
            pairs.append((g * X * Y + tr_of(x + sign * dx, y + sign * dy), g * X * Y + t))
    return lax.ppermute(block, ("grp", "tr"), pairs)


def multiply(blocks, integrals_ref):
    left = jnp.concatenate([block.reshape(-1, block.shape[-1]) for block in blocks], axis=0)
    return jnp.dot(left, integrals_ref[0], preferred_element_type=jnp.float32)


def this_core():
    return lax.rem(lax.axis_index("grp"), 2)


def copy_own(own_ref, copy_ref):
    copy_ref[...] = own_ref[...]


def near_product(own_ref, right_ref, integrals_ref, ours_ref, theirs_ref):
    core = this_core()
    rows = own_ref.shape[1]
    product = multiply([own_ref[...], right_ref[...]], integrals_ref)
    for d in range(2):
        for block in range(8):
            start = (8 * d + block) * rows
            values = product[start : start + rows]
            owner = 0 if block in PLACES[0] else 1
            span = pl.ds(PLACES[owner].index(block) * rows, rows)

            @pl.when(core == owner)
            def _():
                ours_ref[d, span] = values

            @pl.when(core != owner)
            def _():
                theirs_ref[d, span] = values


def far_product(side, left_ref, up_ref, integrals_ref, out_ref):
    core = lax.rem(this_core() + side, 2)
    places = [first + core * (second - first) for first, second in zip(*PLACES)]
    blocks = [ref[place] for ref in (left_ref, up_ref) for place in places]
    product = multiply(blocks, integrals_ref)
    count = out_ref.shape[1]
    out_ref[0] = product[:count]
    out_ref[1] = product[count:]


def pack(near_ours_ref, near_given_ref, far_ours_ref, far_given_ref, out_ref):
    lanes = out_ref.shape[2]
    rows = near_ours_ref.shape[1] // 4
    groups = near_ours_ref.shape[2] // lanes
    ours = [near_ours_ref.at[0], near_ours_ref.at[1], far_ours_ref.at[1], far_ours_ref.at[0]]
    given = [near_given_ref.at[0], near_given_ref.at[1], far_given_ref.at[1], far_given_ref.at[0]]
    odd = lax.rem(lax.axis_index("tr") // Y, 2)
    for way in range(2):

        @pl.when(odd == way)
        def _():
            for d in range(CLASSES):
                for h in range(2):
                    place_out = FOLD.index(2 * d + h)
                    exponents = []
                    for b in range(2):
                        at = (1 - 2 * way) * ((d + 2 * b) % CLASSES)
                        span = pl.ds((2 * b + h) * rows, rows)
                        value = ours[at][span, :] + given[at][span, :]
                        top = jnp.max(jnp.abs(value), axis=1, keepdims=True)
                        exponent = jnp.ceil(FINE * jnp.log2(jnp.maximum(top, 2.0**-110)))
                        scaled = jnp.clip(jnp.round(value * jnp.exp2(15.0 - exponent / FINE)), -32767.0, 32767.0)
                        number = scaled.astype(jnp.int32).astype(jnp.int16)
                        for g in range(groups):
                            lane = pl.ds((2 * g + b) * rows, rows)
                            out_ref[place_out, lane, :] = number[:, g * lanes : (g + 1) * lanes]
                        exponents.append(jnp.broadcast_to(exponent, (rows, lanes)))
                    lower = lax.broadcasted_iota(jnp.int32, (rows, lanes), 1) < lanes // 2
                    both = jnp.where(lower, exponents[0], exponents[1])
                    out_ref[place_out, pl.ds(2 * groups * rows, rows), :] = both.astype(jnp.int32).astype(jnp.int16)


def unpack_sum(in_ref, out_ref):
    planes, _, lanes = in_ref.shape
    rows = out_ref.shape[0] // 2
    groups = out_ref.shape[1] // lanes
    steps = []
    for p in range(planes):
        exponent = in_ref[p, pl.ds(2 * groups * rows, rows), :].astype(jnp.int32).astype(jnp.float32)
        step = jnp.exp2(exponent / FINE - 15.0)
        steps.append((step[:, :1], step[:, lanes // 2 : lanes // 2 + 1]))
    for b in range(2):
        for g in range(groups):
            total = jnp.zeros((rows, lanes), jnp.float32)
            for p in range(planes):
                number = in_ref[p, pl.ds((2 * g + b) * rows, rows), :].astype(jnp.int32).astype(jnp.float32)
                total += number * steps[p][b]
            out_ref[pl.ds(b * rows, rows), g * lanes : (g + 1) * lanes] = total.astype(out_ref.dtype)


LANES = 128
FINE = 64
LIMIT_DOT = 8


def call(kernel, shapes, name, limit, flops=0):
    vmem = pl.BlockSpec(memory_space=pltpu.VMEM)
    single = not isinstance(shapes, tuple)

    def run(*operands):
        moved = sum(x.size * x.dtype.itemsize for x in (*operands, *((shapes,) if single else shapes)))
        return pl.pallas_call(
            kernel,
            out_shape=shapes,
            in_specs=[vmem] * len(operands),
            out_specs=vmem if single else (vmem,) * len(shapes),
            compiler_params=pltpu.CompilerParams(vmem_limit_bytes=limit << 20),
            cost_estimate=pl.CostEstimate(flops=flops, bytes_accessed=moved, transcendentals=0),
            name=name,
        )(*operands)

    return run


def on_device(amplitudes, integrals, slab_count):
    rows, _, depth = amplitudes.shape
    width = integrals.shape[2]
    column = lax.broadcasted_iota(jnp.int32, (rows, depth), 1)
    masked = jnp.where(column < slab_count[0, 0], amplitudes[:, 0, :], jnp.zeros((), amplitudes.dtype))
    copies = jnp.broadcast_to(masked[None], (8, rows, depth))
    own = lax.all_to_all(copies, "tr", 0, 0, axis_index_groups=CLASS_GROUPS)
    right = exchange(own, 1, 0)
    left = exchange(own, -1, 0)
    parts = jax.ShapeDtypeStruct(own.shape, own.dtype)
    copy = call(copy_own, parts, "copy_own", 4, 4000000000)(own)
    up = exchange(copy, 0, 1, 1)

    side = jax.ShapeDtypeStruct((2, 4 * rows, width), jnp.float32)
    work = 2 * 8 * rows * depth * width
    swap = [(g, g ^ 1) for g in range(2 * Z)]
    near, near_theirs = call(near_product, (side, side), "near", LIMIT_DOT, 2 * work)(own, right, integrals)
    near_given = lax.ppermute(near_theirs, "grp", swap)
    far_theirs = call(functools.partial(far_product, 1), side, "far_theirs", LIMIT_DOT, work)(left, up, integrals)
    far_given = lax.ppermute(far_theirs, "grp", swap)
    far = call(functools.partial(far_product, 0), side, "far_ours", LIMIT_DOT, work)(left, up, integrals)
    block = jax.ShapeDtypeStruct((Z, 2 * rows * (width // LANES) + rows, LANES), jnp.int16)
    packed = call(pack, block, "pack", 4)(near, near_given, far, far_given)
    arrived = lax.all_to_all(packed, ("grp", "tr"), 0, 0, axis_index_groups=Z_GROUPS)
    ladder = call(unpack_sum, jax.ShapeDtypeStruct((2 * rows, width), jnp.bfloat16), "unpack_sum", 2)(arrived)
    return ladder[:, None, :]


def solution(mesh):
    return jax.shard_map(
        on_device,
        mesh=mesh,
        in_specs=(P("tr", None, "grp"), P(None, "grp", "tr"), P(None, "grp")),
        out_specs=P("grp", None, "tr"),
        check_vma=False,
    )
```
